256 devices in a mesh: section: 2 (over x_lo), group: 4 (over x_hi, core), mp: 32 (over y, z).
Axes of the slice: x: 4 (x_hi: 2, x_lo: 2; x = x_hi * 2 + x_lo), y: 4, z: 8, core: 2. Of those that a mesh axis runs over, the one named last changes fastest.
Arguments:
- hidden: bfloat16 [2, 3072, 28672], P('section', 'group', 'mp'), may hold values from -6 to 6
- down_weight: bfloat16 [2, 28672, 8192], P('section', 'mp', 'group'), may hold values from -0.0625 to 0.0625
- residual: bfloat16 [2, 3072, 8192], P('section', ('group', 'mp')), may hold values from -12 to 12
- norm_gain: float32 [2, 8192], P('section', 'mp'), may hold values from 0.25 to 1.75
Outputs:
- handed: bfloat16 [2, 3072, 8192], P('section', 'group', 'mp')
- normed: bfloat16 [2, 3072, 8192], P('section', 'group', 'mp')
The draws below stay inside these ranges and needn't reach their ends.
All inputs are finite; a program needn't handle non-finite values.
Results may differ from the reference program's by a relative error of at most 0.017.
Values may be sent and summed in bfloat16 or wider, within the bound.
No kernel may reach another device: no remote copies, remote signals or barrier semaphores. Data moves between devices by JAX's collectives and lax.ppermute only.
A program may use at most 128 MiB of HBM per device.

```python
import jax
import jax.numpy as jnp
from jax import lax

D = 8192
FF = 28672
SECTIONS = 2
ROWS = 3072
N_MP = 32


def draw_residual(key, part):
    column = jnp.arange(D, dtype=jnp.float32) / D
    scale = 0.5 + 1.5 * column
    values = jax.random.normal(key, (SECTIONS, ROWS, D), jnp.float32) * scale
    return jnp.clip(values, -12.0, 12.0).astype(jnp.bfloat16)


def with_spikes(array, stream_key, source, target, parts, factor):
    owner, partner = [(jnp.arange(array.shape[dim]) // (array.shape[dim] // parts)).reshape([-1 if axis == dim else 1 for axis in range(array.ndim)]) for dim in (source, target)]
    chosen = jax.random.permutation(stream_key, parts)[partner]
    strong = (owner == chosen) | (owner == (partner + parts // 2) % parts)
    return jnp.where(strong, factor * array, array)


def shard_levels(key, dims, cuts, low, largest):
    factor_of = 1.0
    for axis_at, parts in cuts:
        draws = jax.random.uniform(jax.random.fold_in(jax.random.fold_in(key, 6), axis_at), (parts,), jnp.float32, low / len(cuts), largest / len(cuts))
        factor_of = factor_of * jnp.repeat(jnp.exp(draws), dims[axis_at] // parts).reshape((-1,) + (1,) * (len(dims) - 1 - axis_at))
    return factor_of


def normal_values(stream_key, extent, deviation, reach, pieces=(), held_as=jnp.bfloat16):
    entries = deviation * jax.random.normal(stream_key, extent, jnp.float32)
    if pieces:
        entries = entries * shard_levels(stream_key, extent, pieces, -0.22, 0.18)
    return jnp.clip(entries, -reach, reach).astype(held_as)


def bell_draw_with(rng, dims, width, most, pieces, heavy, held_as=jnp.bfloat16):
    drawn = width * jax.random.normal(rng, dims, jnp.float32)
    if pieces:
        drawn = drawn * shard_levels(rng, dims, pieces, -0.22, 0.18)
    return jnp.clip(with_spikes(drawn, jax.random.fold_in(rng, 3), *heavy), -most, most).astype(held_as)


def setup_inputs(seed: int = 0) -> dict:
    key_list = jax.random.split(jax.random.key(seed), 5)
    hidden = normal_values(key_list[0], (SECTIONS, ROWS, FF), 1.0, 6.0, ((0, 2), (1, 4), (2, 32)))
    down_weight = bell_draw_with(key_list[1], (SECTIONS, FF, D), FF ** -0.5, 0.0625, ((0, 2), (1, 32), (2, 4)), (1, 2, 32, 2.75))
    residual = draw_residual(jax.random.fold_in(key_list[4], 71), 0)
    norm_gain = jnp.clip(1.0 + 0.15 * jax.random.normal(key_list[3], (SECTIONS, D), jnp.float32), 0.25, 1.75)
    return dict(hidden=hidden, down_weight=down_weight, residual=residual, norm_gain=norm_gain)


def section_stream(hid, weight, resid):
    blocks = FF // N_MP
    hid_blocks = hid.reshape(ROWS, N_MP, blocks).transpose(1, 0, 2)
    weight_blocks = weight.reshape(N_MP, blocks, D)

    def add_block(total, pair):
        term = jnp.dot(pair[0], pair[1], preferred_element_type=jnp.float32).astype(jnp.bfloat16)
        term = lax.optimization_barrier(term)
        return (total + term.astype(jnp.float32), None)
    total, unused = lax.scan(add_block, jnp.zeros((ROWS, D), jnp.float32), (hid_blocks, weight_blocks))
    return (resid.astype(jnp.float32) + total).astype(jnp.bfloat16)

def reference(hidden, down_weight, residual, norm_gain):
    streams = jnp.stack([section_stream(hidden[s], down_weight[s], residual[s]) for s in range(SECTIONS)])
    handed = jnp.roll(streams, 1, axis=0)
    values = handed.astype(jnp.float32)
    meansq = lax.optimization_barrier(jnp.mean(values * values, axis=2, keepdims=True))
    normed = (values * lax.rsqrt(meansq + 1e-05) * norm_gain[:, None, :]).astype(jnp.bfloat16)
    return (handed, normed)
```

```python
import jax
import jax.numpy as jnp
from jax import lax
from jax.sharding import Mesh
from jax.sharding import PartitionSpec as P

D = 8192
NZ, NY = 8, 4
ROWS, COLS = 768, 256
ZROWS = 320
AXES = ("s", "xh", "c", "y", "z")
F32, BF16 = jnp.float32, jnp.bfloat16


def shifted(x, axis, n, by):
    return lax.ppermute(x, axis, [(i, (i + by) % n) for i in range(n)])


def flipped(x, *axes):
    n = 2 ** len(axes)
    return lax.ppermute(x, axes, [(i, n - 1 - i) for i in range(n)])


def ring_sum(piece, axis, n, cut):
    far = piece(n // 2)
    half = far.shape[cut] // 2
    low, high = (lax.slice_in_dim(far, i * half, (i + 1) * half, axis=cut) for i in (0, 1))
    up, down = shifted(low, axis, n, 1), shifted(high, axis, n, -1)
    for j in range(n // 2 - 1, 0, -1):
        ahead, behind = piece(j), piece(-j)
        if up.shape != ahead.shape:
            parts = [lax.slice_in_dim(ahead, i * half, (i + 1) * half, axis=cut) for i in (0, 1)]
            ahead = jnp.concatenate([parts[0] + up, parts[1]], axis=cut)
            parts = [lax.slice_in_dim(behind, i * half, (i + 1) * half, axis=cut) for i in (0, 1)]
            behind = jnp.concatenate([parts[0], parts[1] + down], axis=cut)
        else:
            ahead, behind = ahead + up, behind + down
        up, down = shifted(ahead, axis, n, 1), shifted(behind, axis, n, -1)
    return piece(0).astype(F32) + up.astype(F32) + down.astype(F32)


def by_columns(x, z):
    return lambda j: lax.dynamic_slice_in_dim(x, (z + j) % NZ * COLS, COLS, axis=1)


def by_rows(x, y):
    rows = x.shape[0] // NY
    return lambda j: lax.dynamic_slice_in_dim(x, (y + j) % NY * rows, rows, axis=0)


def scattered(h, w, res, y, z):
    partial = jnp.dot(h, w, preferred_element_type=F32).astype(BF16)
    at = (y * NZ + z) * res.shape[0]
    slab = lax.dynamic_slice_in_dim(partial, at, res.shape[0], axis=0)
    partial = lax.dynamic_update_slice_in_dim(partial, slab + res, at, axis=0)
    z_sum = ring_sum(by_columns(partial[:ZROWS], z), "z", NZ, 0).astype(BF16)
    y_sum = ring_sum(by_rows(partial[ZROWS:], y), "y", NY, 1).astype(BF16)
    z_first = ring_sum(by_rows(z_sum, y), "y", NY, 1)
    y_first = ring_sum(by_columns(y_sum, z), "z", NZ, 1)
    return jnp.concatenate([z_first, y_first], axis=0).astype(BF16)


def across(by):
    pairs = []
    for i in range(2 * 4 * NY * NZ):
        s, g, y, z = i // 128, i // 32 % 4, i // 8 % 4, i % 8
        pairs.append((i, (1 - s) * 128 + (y + by) % 4 * 32 + g * 8 + z))
    return pairs


def shards(hidden, down_weight, residual, norm_gain):
    h, w, gain = hidden[0], down_weight[0], norm_gain[0]
    xh, c, y, z = (lax.axis_index(a) for a in AXES[1:])
    group = xh * 2 + c
    h_core = flipped(h, "c")
    zero = c == 0
    got = [
        lax.ppermute(h, ("xh", "c"), [(k, 2 + k), (2 + k, k)]) for k in (0, 1)
    ]
    h_far = [
        jnp.where(c == k, got[k], lax.ppermute(got[k], "c", [(k, 1 - k)])) for k in (0, 1)
    ]
    res = residual[0].reshape(24, 4, 2048)
    part = lambda r: lax.dynamic_index_in_dim(res, group ^ r, axis=1, keepdims=False)
    res_near = [part(0), flipped(part(1), "c")]
    far = [flipped(part(2), "xh"), flipped(part(3), "xh", "c")]
    res_far = [jnp.where(zero, far[0], far[1]), jnp.where(zero, far[1], far[0])]
    blocks = [
        scattered(a, w, r, y, z)
        for a, r in zip([h, h_core] + h_far, res_near + res_far)
    ]
    stack = jnp.stack(blocks)
    place = [jnp.where(xh == g // 2, (c + g) % 2, 2 + g % 2) for g in range(4)]
    stream = jnp.stack(
        [lax.dynamic_index_in_dim(stack, p, axis=0, keepdims=False) for p in place]
    )
    wide = stream.astype(F32)
    squares = jnp.sum(wide * wide, axis=2)
    squares = squares + flipped(squares, "c") + flipped(squares, "xh") + flipped(squares, "xh", "c")
    squares = sum([shifted(squares, "z", NZ, j) for j in range(1, NZ)], squares)

    def hand(x):
        sent = [
            lax.ppermute(
                lax.dynamic_index_in_dim(x, (y + by) % 4, axis=0, keepdims=False),
                AXES,
                across(by),
            )
            for by in range(4)
        ]
        sent = jnp.stack(sent)
        quarters = [
            lax.dynamic_index_in_dim(sent, (group - q) % 4, axis=0, keepdims=False)
            for q in range(4)
        ]
        cut = ZROWS // 4
        return jnp.concatenate([q[:cut] for q in quarters] + [q[cut:] for q in quarters])

    handed = hand(stream)
    scale = lax.rsqrt(hand(squares) / D + 1e-05)
    normed = (handed.astype(F32) * scale[:, None] * gain[None, :]).astype(BF16)
    return (handed[None], normed[None])


def solution(mesh):
    fine = Mesh(mesh.devices.reshape(2, 2, 2, NY, NZ), AXES)
    group, mp = ("xh", "c"), ("y", "z")
    return jax.shard_map(
        shards,
        mesh=fine,
        in_specs=(P("s", group, mp), P("s", mp, group), P("s", group + mp, None), P("s", mp)),
        out_specs=(P("s", group, mp), P("s", group, mp)),
        check_vma=False,
    )
```

```python
import functools

import jax
import jax.numpy as jnp
from jax import lax
from jax.experimental import pallas as pl
from jax.experimental.pallas import tpu as pltpu
from jax.sharding import Mesh
from jax.sharding import PartitionSpec as P

D = 8192
NZ, NY = 8, 4
COLS = 256
HALF = 384
ORDER = ((0, 192), (192, HALF))
SCALE, FAR = 1, 100
VMEM = 58 * 2**20
AXES = ("s", "xh", "c", "y", "z")
F32, BF16 = jnp.float32, jnp.bfloat16


def shifted(x, axis, n, by):
    return lax.ppermute(x, axis, [(i, (i + by) % n) for i in range(n)])


def flipped(x, *axes):
    n = 2 ** len(axes)
    return lax.ppermute(x, axes, [(i, n - 1 - i) for i in range(n)])


def product_kernel(first, rows, y_major, m_ref, h0_ref, h1_ref, w_ref, r0_ref, r1_ref, *refs):
    out_ref = refs[-1]

    def block(i, half):
        return (i * 2 + half, 0) if y_major else (0, i * 2 + half)

    for i, h_ref in enumerate((h0_ref, h1_ref)):
        for half in range(2):
            at = half * rows
            acc = jnp.dot(h_ref[at : at + rows], w_ref[...], preferred_element_type=F32)
            out_ref[block(i, half)] = acc.astype(BF16)

    m = m_ref[0]
    row = m % 16 * 24

    @pl.when((row >= first) & (row < first + rows))
    def _():
        window = pl.ds(pl.multiple_of(row // 16 * 16 - first, 16), 32)
        for i, r_ref in enumerate((r0_ref, r1_ref)):
            at = block(i, m // 16) + (window, slice(None))
            out_ref[at] = (out_ref[at].astype(F32) + r_ref[...].astype(F32)).astype(BF16)


def product(m, h, w, res, first, rows, y_major, scale=1, after=()):
    whole = lambda j: (0, 0)
    columns = lambda j: (0, j)
    if y_major:
        shape, block, place = (NY, NZ, rows, COLS), (NY, 1, rows, COLS), lambda j: (0, j, 0, 0)
    else:
        shape, block, place = (NZ, NY, rows, COLS), (1, NY, rows, COLS), lambda j: (j, 0, 0, 0)
    return pl.pallas_call(
        functools.partial(product_kernel, first, rows, y_major),
        out_shape=jax.ShapeDtypeStruct(shape, BF16),
        grid=(NZ,),
        in_specs=[
            pl.BlockSpec(memory_space=pltpu.SMEM),
            pl.BlockSpec(h[0].shape, whole),
            pl.BlockSpec(h[1].shape, whole),
            pl.BlockSpec((w.shape[0], COLS), columns),
            pl.BlockSpec((32, COLS), columns),
            pl.BlockSpec((32, COLS), columns),
        ]
        + [pl.BlockSpec(memory_space=pl.ANY)] * len(after),
        out_specs=pl.BlockSpec(block, place),
        compiler_params=pltpu.CompilerParams(vmem_limit_bytes=VMEM),
        cost_estimate=pl.CostEstimate(
            flops=scale * 2 * NY * rows * w.size,
            bytes_accessed=2 * (NY * rows * NZ * COLS + w.size + 2 * h[0].size),
            transcendentals=0,
        ),
    )(m, h[0], h[1], w, res[0], res[1], *after)


def tied(x, *after):
    anywhere = pl.BlockSpec(memory_space=pl.ANY)
    return pl.pallas_call(
        lambda *refs: None,
        out_shape=jax.ShapeDtypeStruct(x.shape, x.dtype),
        in_specs=[anywhere] * (1 + len(after)),
        out_specs=anywhere,
        input_output_aliases={0: 0},
    )(x, *after)


def summed_along_y(x, y):
    half = x.shape[1] // 2
    take = lambda j: lax.dynamic_index_in_dim(x, (y + j) % NY, axis=0, keepdims=False)
    far, ahead, behind = take(2), take(1), take(-1)
    up, down = shifted(far[:half], "y", NY, 1), shifted(far[half:], "y", NY, -1)
    ahead = jnp.concatenate([ahead[:half] + up, ahead[half:]])
    behind = jnp.concatenate([behind[:half], behind[half:] + down])
    up, down = shifted(ahead, "y", NY, 1), shifted(behind, "y", NY, -1)
    return take(0).astype(F32) + up.astype(F32) + down.astype(F32)


def summed_along_z(x):
    return lax.psum_scatter(x, "z", scatter_dimension=0, tiled=False)


def handing(odd):
    pairs = []
    for i in range(2 * 4 * NY * NZ):
        s, g, y, z = i // 128, i // 32 % 4, i // 8 % 4, i % 8
        pairs.append((i, (1 - s) * 128 + (g ^ (y // 2) ^ (2 * ((y + odd) % 2))) * 32 + g * 8 + z))
    return pairs


def handed_over(pair, group, y):
    swapped = y % 2 == 1
    one = jnp.where(swapped, pair[1], pair[0])
    two = jnp.where(swapped, pair[0], pair[1])
    one = lax.ppermute(one, AXES, handing(0))
    two = lax.ppermute(two, AXES, handing(1))
    turned = (group ^ y) >= 2
    return jnp.concatenate([jnp.where(turned, two, one), jnp.where(turned, one, two)])


def shards(hidden, down_weight, residual, norm_gain):
    h, w, gain = hidden[0], down_weight[0], norm_gain[0]
    xh, c, y, z = (lax.axis_index(a) for a in AXES[1:])
    group = xh * 2 + c
    res = residual[0].reshape(24, 4, 2048)
    part = lambda x, r: lax.dynamic_index_in_dim(x, group ^ r, axis=1, keepdims=False)
    got = flipped(jnp.stack([part(res, 1), part(res, 3)]), "c")
    far = flipped(jnp.stack([part(res, 2), got[1]]), "xh")
    m = y * NZ + z
    pad = lambda x: jnp.where(m % 2 == 0, jnp.pad(x, ((0, 8), (0, 0))), jnp.pad(x, ((8, 0), (0, 0))))
    near_res = (pad(part(res, 0)), pad(got[0]))
    far_res = (pad(far[0]), pad(far[1]))
    m = m.reshape(1)
    core = flipped(h, "c")
    product_near = product(m, (h, core), w, near_res, 0, HALF, False, SCALE)
    near = summed_along_y(summed_along_z(product_near), y).astype(BF16)
    sums, last = [], product_near
    for a, b in ORDER:
        x = h.reshape(2, HALF, -1)[:, a:b].reshape(2 * (b - a), -1)
        x = flipped(tied(x, near_res[1]) if a else x, "xh")
        x = tied(x, last)
        x = last = product(m, (x, flipped(x, "c")), w, far_res, a, b - a, True, 1 if a else FAR)
        x = summed_along_y(x, y).astype(BF16)
        x = lax.all_to_all(x, "z", split_axis=0, concat_axis=0, tiled=True)
        sums.append(jnp.sum(x.astype(F32), axis=0).astype(BF16))
    handed = handed_over((near, jnp.concatenate(sums)), group, y)
    wide = handed.astype(F32)
    squares = jnp.sum(wide * wide, axis=1)
    squares = lax.all_to_all(
        jnp.broadcast_to(squares, (NY * NZ, 768)), ("y", "z"), split_axis=0, concat_axis=0, tiled=True
    )
    scale = lax.rsqrt(jnp.sum(squares, axis=0) / D + 1e-05)
    normed = (wide * scale[:, None] * gain[None, :]).astype(BF16)
    return (handed[None], normed[None])


def solution(mesh):
    fine = Mesh(mesh.devices.reshape(2, 2, 2, NY, NZ), AXES)
    group, mp = ("xh", "c"), ("y", "z")
    return jax.shard_map(
        shards,
        mesh=fine,
        in_specs=(P("s", group, mp), P("s", mp, group), P("s", group + mp, None), P("s", mp)),
        out_specs=(P("s", group, mp), P("s", group, mp)),
        check_vma=False,
    )
```

```python
import functools

import jax
import jax.numpy as jnp
from jax import lax
from jax.experimental import pallas as pl
from jax.experimental.pallas import tpu as pltpu
from jax.sharding import Mesh
from jax.sharding import PartitionSpec as P

D = 8192
NZ, NY = 8, 4
COLS = 256
STEP = 2
HALF = 384
ORDER = ((0, 192), (192, HALF))
TIE = 3 * 10**11
SCALE, FAR = 20, 1
VMEM = 58 * 2**20
AXES = ("s", "xh", "c", "y", "z")
F32, BF16 = jnp.float32, jnp.bfloat16


def shifted(x, axis, n, by):
    return lax.ppermute(x, axis, [(i, (i + by) % n) for i in range(n)])


def flipped(x, *axes):
    n = 2 ** len(axes)
    return lax.ppermute(x, axes, [(i, n - 1 - i) for i in range(n)])


def product_kernel(first, rows, y_major, m_ref, h0_ref, h1_ref, w_ref, r0_ref, r1_ref, *refs):
    out_ref = refs[-1]

    def block(i, half, k):
        return (i * 2 + half, k) if y_major else (k, i * 2 + half)

    parts = [slice(k * COLS, (k + 1) * COLS) for k in range(STEP)]
    for i, h_ref in enumerate((h0_ref, h1_ref)):
        for half in range(2):
            at = half * rows
            acc = jnp.dot(h_ref[at : at + rows], w_ref[...], preferred_element_type=F32)
            for k, part in enumerate(parts):
                out_ref[block(i, half, k)] = acc[:, part].astype(BF16)

    m = m_ref[0]
    row = m % 16 * 24

    @pl.when((row >= first) & (row < first + rows))
    def _():
        window = pl.ds(pl.multiple_of(row // 16 * 16 - first, 16), 32)
        for i, r_ref in enumerate((r0_ref, r1_ref)):
            none = jnp.zeros((8, COLS), F32)
            for k, part in enumerate(parts):
                r = r_ref[:, part].astype(F32)
                late, soon = jnp.concatenate([none, r]), jnp.concatenate([r, none])
                at = block(i, m // 16, k) + (window, slice(None))
                out_ref[at] = (out_ref[at].astype(F32) + jnp.where(row % 16 == 8, late, soon)).astype(BF16)


def product(m, h, w, res, first, rows, y_major, scale=1, after=()):
    whole = lambda j: (0, 0)
    columns = lambda j: (0, j)
    if y_major:
        shape, block, place = (NY, NZ, rows, COLS), (NY, STEP, rows, COLS), lambda j: (0, j, 0, 0)
    else:
        shape, block, place = (NZ, NY, rows, COLS), (STEP, NY, rows, COLS), lambda j: (j, 0, 0, 0)
    return pl.pallas_call(
        functools.partial(product_kernel, first, rows, y_major),
        out_shape=jax.ShapeDtypeStruct(shape, BF16),
        grid=(NZ // STEP,),
        in_specs=[
            pl.BlockSpec(memory_space=pltpu.SMEM),
            pl.BlockSpec(h[0].shape, whole),
            pl.BlockSpec(h[1].shape, whole),
            pl.BlockSpec((w.shape[0], STEP * COLS), columns),
            pl.BlockSpec((24, STEP * COLS), columns),
            pl.BlockSpec((24, STEP * COLS), columns),
        ]
        + [pl.BlockSpec(memory_space=pl.ANY)] * len(after),
        out_specs=pl.BlockSpec(block, place),
        compiler_params=pltpu.CompilerParams(vmem_limit_bytes=VMEM),
        cost_estimate=pl.CostEstimate(
            flops=scale * 2 * NY * rows * w.size,
            bytes_accessed=2 * (NY * rows * NZ * COLS + w.size + 2 * h[0].size),
            transcendentals=0,
        ),
    )(m, h[0], h[1], w, res[0], res[1], *after)


def tied(x, *after, flops=0):
    anywhere = pl.BlockSpec(memory_space=pl.ANY)
    return pl.pallas_call(
        lambda *refs: None,
        out_shape=jax.ShapeDtypeStruct(x.shape, x.dtype),
        in_specs=[anywhere] * (1 + len(after)),
        out_specs=anywhere,
        input_output_aliases={0: 0},
        cost_estimate=pl.CostEstimate(flops=flops, bytes_accessed=0, transcendentals=0),
    )(x, *after)


def summed_along_y(x, y):
    half = x.shape[1] // 2
    take = lambda j: lax.dynamic_index_in_dim(x, (y + j) % NY, axis=0, keepdims=False)
    far, ahead, behind = take(2), take(1), take(-1)
    up, down = shifted(far[:half], "y", NY, 1), shifted(far[half:], "y", NY, -1)
    ahead = jnp.concatenate([ahead[:half] + up, ahead[half:]])
    behind = jnp.concatenate([behind[:half], behind[half:] + down])
    up, down = shifted(ahead, "y", NY, 1), shifted(behind, "y", NY, -1)
    return take(0).astype(F32) + up.astype(F32) + down.astype(F32)


def summed_along_z(x):
    return lax.psum_scatter(x, "z", scatter_dimension=0, tiled=False)


def handing(odd):
    pairs = []
    for i in range(2 * 4 * NY * NZ):
        s, g, y, z = i // 128, i // 32 % 4, i // 8 % 4, i % 8
        pairs.append((i, (1 - s) * 128 + (g ^ (y // 2) ^ (2 * ((y + odd) % 2))) * 32 + g * 8 + z))
    return pairs


def handed_over(pair, group, y):
    swapped = y % 2 == 1
    one = jnp.where(swapped, pair[1], pair[0])
    two = jnp.where(swapped, pair[0], pair[1])
    one = lax.ppermute(one, AXES, handing(0))
    two = lax.ppermute(two, AXES, handing(1))
    turned = (group ^ y) >= 2
    return jnp.concatenate([jnp.where(turned, two, one), jnp.where(turned, one, two)])


def shards(hidden, down_weight, residual, norm_gain):
    h, w, gain = hidden[0], down_weight[0], norm_gain[0]
    xh, c, y, z = (lax.axis_index(a) for a in AXES[1:])
    group = xh * 2 + c
    part = lambda r: lax.dynamic_slice_in_dim(residual[0], (group ^ r) * 2048, 2048, axis=1)
    got = flipped(jnp.stack([part(1), part(3)]), "c")
    far_res = jnp.stack([part(2), got[1]])
    near_res = (part(0), got[0])
    m = y * NZ + z
    m = m.reshape(1)
    core = flipped(h, "c")
    product_near = product(m, (h, core), w, near_res, 0, HALF, False, SCALE)
    far_res = flipped(far_res, "xh")
    near = summed_along_y(summed_along_z(product_near), y).astype(BF16)
    sums, last = [], product_near
    for a, b in ORDER:
        x = h.reshape(2, HALF, -1)[:, a:b].reshape(2 * (b - a), -1)
        x = flipped(tied(x, near_res[1]) if a else x, "xh")
        x = tied(x, last, flops=0 if a else TIE)
        x = last = product(m, (x, flipped(x, "c")), w, far_res, a, b - a, True, 1 if a else FAR)
        x = summed_along_y(x, y).astype(BF16)
        x = lax.all_to_all(x, "z", split_axis=0, concat_axis=0, tiled=True)
        sums.append(jnp.sum(x.astype(F32), axis=0).astype(BF16))
    handed = handed_over((near, jnp.concatenate(sums)), group, y)
    wide = handed.astype(F32)
    squares = jnp.sum(wide * wide, axis=1)
    squares = lax.all_to_all(
        jnp.broadcast_to(squares, (NY * NZ, 768)), ("y", "z"), split_axis=0, concat_axis=0, tiled=True
    )
    scale = lax.rsqrt(jnp.sum(squares, axis=0) / D + 1e-05)
    normed = (wide * scale[:, None] * gain[None, :]).astype(BF16)
    return (handed[None], normed[None])


def solution(mesh):
    fine = Mesh(mesh.devices.reshape(2, 2, 2, NY, NZ), AXES)
    group, mp = ("xh", "c"), ("y", "z")
    return jax.shard_map(
        shards,
        mesh=fine,
        in_specs=(P("s", group, mp), P("s", mp, group), P("s", group + mp, None), P("s", mp)),
        out_specs=(P("s", group, mp), P("s", group, mp)),
        check_vma=False,
    )
```

```python
import functools

import jax
import jax.numpy as jnp
from jax import lax
from jax.experimental import pallas as pl
from jax.experimental.pallas import tpu as pltpu
from jax.sharding import Mesh
from jax.sharding import PartitionSpec as P

D = 8192
NZ, NY = 8, 4
COLS = 256
STEP = 2
HALF = 384
ORDER = ((0, 192), (192, HALF))
TIE = 3 * 10**11
SCALE, FAR = 20, 1
VMEM = 58 * 2**20
AXES = ("s", "xh", "c", "y", "z")
F32, BF16 = jnp.float32, jnp.bfloat16


def shifted(x, axis, n, by):
    return lax.ppermute(x, axis, [(i, (i + by) % n) for i in range(n)])


def flipped(x, *axes):
    n = 2 ** len(axes)
    return lax.ppermute(x, axes, [(i, n - 1 - i) for i in range(n)])


def product_kernel(first, rows, relative, m_ref, h0_ref, h1_ref, w_ref, r0_ref, r1_ref, *out_refs):
    m = m_ref[0]
    step = pl.program_id(0)
    parts = [slice(k * COLS, (k + 1) * COLS) for k in range(STEP)]

    def at_owner(owner, k, use):
        if not relative:
            use(out_refs[0], (k, owner))
            return
        low_ref, high_ref, rest_ref = out_refs
        ahead = lax.rem(owner - m // NZ + NY, NY)
        pl.when(ahead != 2)(lambda: use(rest_ref, (jnp.where(ahead == 3, 2, ahead), k)))
        early = step < NZ // STEP // 2
        pl.when((ahead == 2) & early)(lambda: use(low_ref, (k,)))
        pl.when((ahead == 2) & jnp.logical_not(early))(lambda: use(high_ref, (k,)))

    for i, h_ref in enumerate((h0_ref, h1_ref)):
        acc = jnp.dot(h_ref[...], w_ref[...], preferred_element_type=F32).astype(BF16)
        for half in range(2):
            for k, part in enumerate(parts):

                def store(ref, at, value=acc[half * rows : (half + 1) * rows, part]):
                    ref[at] = value

                at_owner(i * 2 + half, k, store)

    row = m % 16 * 24

    @pl.when((row >= first) & (row < first + rows))
    def _():
        window = pl.ds(pl.multiple_of(row // 16 * 16 - first, 16), 32)
        for i, r_ref in enumerate((r0_ref, r1_ref)):
            none = jnp.zeros((8, COLS), F32)
            for k, part in enumerate(parts):
                r = r_ref[:, part].astype(F32)
                late, soon = jnp.concatenate([none, r]), jnp.concatenate([r, none])

                def add(ref, at, value=jnp.where(row % 16 == 8, late, soon)):
                    at = at + (window, slice(None))
                    ref[at] = (ref[at].astype(F32) + value).astype(BF16)

                at_owner(i * 2 + m // 16, k, add)


def product(m, h, w, res, first, rows, relative, scale=1):
    whole = lambda j: (0, 0)
    columns = lambda j: (0, j)
    if relative:
        last = NZ // STEP // 2 - 1
        out = [
            ((NZ // 2, rows, COLS), (STEP, rows, COLS), lambda j: (jnp.minimum(j, last), 0, 0)),
            ((NZ // 2, rows, COLS), (STEP, rows, COLS), lambda j: (jnp.maximum(j - last - 1, 0), 0, 0)),
            ((3, NZ, rows, COLS), (3, STEP, rows, COLS), lambda j: (0, j, 0, 0)),
        ]
    else:
        out = [((NZ, NY, rows, COLS), (STEP, NY, rows, COLS), lambda j: (j, 0, 0, 0))]
    return pl.pallas_call(
        functools.partial(product_kernel, first, rows, relative),
        out_shape=[jax.ShapeDtypeStruct(shape, BF16) for shape, _, _ in out],
        grid=(NZ // STEP,),
        in_specs=[
            pl.BlockSpec(memory_space=pltpu.SMEM),
            pl.BlockSpec(h[0].shape, whole),
            pl.BlockSpec(h[1].shape, whole),
            pl.BlockSpec((w.shape[0], STEP * COLS), columns),
            pl.BlockSpec((24, STEP * COLS), columns),
            pl.BlockSpec((24, STEP * COLS), columns),
        ],
        out_specs=[pl.BlockSpec(block, place) for _, block, place in out],
        compiler_params=pltpu.CompilerParams(vmem_limit_bytes=VMEM),
        cost_estimate=pl.CostEstimate(
            flops=scale * 2 * NY * rows * w.size,
            bytes_accessed=2 * (NY * rows * NZ * COLS + w.size + 2 * h[0].size),
            transcendentals=0,
        ),
    )(m, h[0], h[1], w, res[0], res[1])


def tied(x, *after, flops=0):
    anywhere = pl.BlockSpec(memory_space=pl.ANY)
    return pl.pallas_call(
        lambda *refs: None,
        out_shape=jax.ShapeDtypeStruct(x.shape, x.dtype),
        in_specs=[anywhere] * (1 + len(after)),
        out_specs=anywhere,
        input_output_aliases={0: 0},
        cost_estimate=pl.CostEstimate(flops=flops, bytes_accessed=0, transcendentals=0),
    )(x, *after)


def summed_along_y(low, high, own, ahead, behind):
    half = low.shape[0]
    up, down = shifted(low, "y", NY, 1), shifted(high, "y", NY, -1)
    ahead = jnp.concatenate([ahead[:half] + up, ahead[half:]])
    behind = jnp.concatenate([behind[:half], behind[half:] + down])
    up, down = shifted(ahead, "y", NY, 1), shifted(behind, "y", NY, -1)
    return own.astype(F32) + up.astype(F32) + down.astype(F32)


def summed_along_z(x):
    return lax.psum_scatter(x, "z", scatter_dimension=0, tiled=False)


def handing(odd):
    pairs = []
    for i in range(2 * 4 * NY * NZ):
        s, g, y, z = i // 128, i // 32 % 4, i // 8 % 4, i % 8
        pairs.append((i, (1 - s) * 128 + (g ^ (y // 2) ^ (2 * ((y + odd) % 2))) * 32 + g * 8 + z))
    return pairs


def handed_over(pair, group, y):
    swapped = y % 2 == 1
    one = jnp.where(swapped, pair[1], pair[0])
    two = jnp.where(swapped, pair[0], pair[1])
    one = lax.ppermute(one, AXES, handing(0))
    two = lax.ppermute(two, AXES, handing(1))
    turned = (group ^ y) >= 2
    return jnp.concatenate([jnp.where(turned, two, one), jnp.where(turned, one, two)])


def shards(hidden, down_weight, residual, norm_gain):
    h, w, gain = hidden[0], down_weight[0], norm_gain[0]
    xh, c, y, z = (lax.axis_index(a) for a in AXES[1:])
    group = xh * 2 + c
    part = lambda r: lax.dynamic_slice_in_dim(residual[0], (group ^ r) * 2048, 2048, axis=1)
    got = flipped(jnp.stack([part(1), part(3)]), "c")
    far_res = jnp.stack([part(2), got[1]])
    near_res = (part(0), got[0])
    m = y * NZ + z
    m = m.reshape(1)
    core = flipped(h, "c")
    (product_near,) = product(m, (h, core), w, near_res, 0, HALF, False, SCALE)
    far_res = flipped(far_res, "xh")
    near = summed_along_z(product_near)
    take = lambda j: lax.dynamic_index_in_dim(near, (y + j) % NY, axis=0, keepdims=False)
    opposite = take(2)
    near = summed_along_y(opposite[: HALF // 2], opposite[HALF // 2 :], take(0), take(1), take(-1))
    near = near.astype(BF16)
    sums, last = [], (product_near, far_res)
    for a, b in ORDER:
        x = h.reshape(2, HALF, -1)[:, a:b].reshape(2 * (b - a), -1)
        x = flipped(tied(x, near_res[1]) if a else x, "xh")
        x = tied(x, *last, flops=0 if a else TIE)
        low, high, rest = product(m, (x, flipped(x, "c")), w, far_res, a, b - a, True, 1 if a else FAR)
        last = (rest,)
        x = summed_along_y(low, high, *rest).astype(BF16)
        x = lax.all_to_all(x, "z", split_axis=0, concat_axis=0, tiled=True)
        sums.append(jnp.sum(x.astype(F32), axis=0).astype(BF16))
    handed = handed_over((near, jnp.concatenate(sums)), group, y)
    wide = handed.astype(F32)
    squares = jnp.sum(wide * wide, axis=1)
    for axis, n in (("z", NZ), ("y", NY)):
        squares = jnp.broadcast_to(squares, (n, 768))
        squares = lax.all_to_all(squares, axis, split_axis=0, concat_axis=0, tiled=True)
        squares = jnp.sum(squares, axis=0)
    scale = lax.rsqrt(squares / D + 1e-05)
    normed = (wide * scale[:, None] * gain[None, :]).astype(BF16)
    return (handed[None], normed[None])


def solution(mesh):
    fine = Mesh(mesh.devices.reshape(2, 2, 2, NY, NZ), AXES)
    group, mp = ("xh", "c"), ("y", "z")
    return jax.shard_map(
        shards,
        mesh=fine,
        in_specs=(P("s", group, mp), P("s", mp, group), P("s", group + mp, None), P("s", mp)),
        out_specs=(P("s", group, mp), P("s", group, mp)),
        check_vma=False,
    )
```

```python
import functools

import jax
import jax.numpy as jnp
from jax import lax
from jax.experimental import pallas as pl
from jax.experimental.pallas import tpu as pltpu
from jax.sharding import Mesh
from jax.sharding import PartitionSpec as P

D = 8192
NZ, NY = 8, 4
COLS = 256
STEP = 2
HALF = 384
ORDER = ((0, 192), (192, HALF))
HOLD = 4 * 10**10
TIE = 3 * 10**11
SCALE, FAR = 20, 1
VMEM = 50 * 2**20
AXES = ("s", "xh", "c", "y", "z")
F32, BF16 = jnp.float32, jnp.bfloat16


def shifted(x, axis, n, by):
    return lax.ppermute(x, axis, [(i, (i + by) % n) for i in range(n)])


def flipped(x, *axes):
    n = 2 ** len(axes)
    return lax.ppermute(x, axes, [(i, n - 1 - i) for i in range(n)])


def product_kernel(first, rows, relative, m_ref, h0_ref, h1_ref, w_ref, r0_ref, r1_ref, *out_refs):
    m = m_ref[0]
    step = pl.program_id(0)
    parts = [slice(k * COLS, (k + 1) * COLS) for k in range(STEP)]

    def at_owner(owner, k, use):
        if not relative:
            use(out_refs[0], (k, owner))
            return
        low_ref, high_ref, rest_ref = out_refs
        ahead = lax.rem(owner - m // NZ + NY, NY)
        pl.when(ahead != 2)(lambda: use(rest_ref, (jnp.where(ahead == 3, 2, ahead), k)))
        early = step < NZ // STEP // 2
        pl.when((ahead == 2) & early)(lambda: use(low_ref, (k,)))
        pl.when((ahead == 2) & jnp.logical_not(early))(lambda: use(high_ref, (k,)))

    for i, h_ref in enumerate((h0_ref, h1_ref)):
        acc = jnp.dot(h_ref[...], w_ref[...], preferred_element_type=F32).astype(BF16)
        for half in range(2):
            for k, part in enumerate(parts):

                def store(ref, at, value=acc[half * rows : (half + 1) * rows, part]):
                    ref[at] = value

                at_owner(i * 2 + half, k, store)

    row = m % 16 * 24

    @pl.when((row >= first) & (row < first + rows))
    def _():
        window = pl.ds(pl.multiple_of(row // 16 * 16 - first, 16), 32)
        for i, r_ref in enumerate((r0_ref, r1_ref)):
            none = jnp.zeros((8, COLS), F32)
            for k, part in enumerate(parts):
                r = r_ref[:, part].astype(F32)
                late, soon = jnp.concatenate([none, r]), jnp.concatenate([r, none])

                def add(ref, at, value=jnp.where(row % 16 == 8, late, soon)):
                    at = at + (window, slice(None))
                    ref[at] = (ref[at].astype(F32) + value).astype(BF16)

                at_owner(i * 2 + m // 16, k, add)


def product(m, h, w, res, first, rows, relative, scale=1):
    whole = lambda j: (0, 0)
    columns = lambda j: (0, j)
    if relative:
        last = NZ // STEP // 2 - 1
        out = [
            ((NZ // 2, rows, COLS), (STEP, rows, COLS), lambda j: (jnp.minimum(j, last), 0, 0)),
            ((NZ // 2, rows, COLS), (STEP, rows, COLS), lambda j: (jnp.maximum(j - last - 1, 0), 0, 0)),
            ((3, NZ, rows, COLS), (3, STEP, rows, COLS), lambda j: (0, j, 0, 0)),
        ]
    else:
        out = [((NZ, NY, rows, COLS), (STEP, NY, rows, COLS), lambda j: (j, 0, 0, 0))]
    return pl.pallas_call(
        functools.partial(product_kernel, first, rows, relative),
        out_shape=[jax.ShapeDtypeStruct(shape, BF16) for shape, _, _ in out],
        grid=(NZ // STEP,),
        in_specs=[
            pl.BlockSpec(memory_space=pltpu.SMEM),
            pl.BlockSpec(h[0].shape, whole),
            pl.BlockSpec(h[1].shape, whole),
            pl.BlockSpec((w.shape[0], STEP * COLS), columns),
            pl.BlockSpec((24, STEP * COLS), columns),
            pl.BlockSpec((24, STEP * COLS), columns),
        ],
        out_specs=[pl.BlockSpec(block, place) for _, block, place in out],
        compiler_params=pltpu.CompilerParams(vmem_limit_bytes=VMEM),
        cost_estimate=pl.CostEstimate(
            flops=scale * 2 * NY * rows * w.size,
            bytes_accessed=2 * (NY * rows * NZ * COLS + w.size + 2 * h[0].size),
            transcendentals=0,
        ),
    )(m, h[0], h[1], w, res[0], res[1])


def tied(x, *after, flops=0):
    anywhere = pl.BlockSpec(memory_space=pl.ANY)
    return pl.pallas_call(
        lambda *refs: None,
        out_shape=jax.ShapeDtypeStruct(x.shape, x.dtype),
        in_specs=[anywhere] * (1 + len(after)),
        out_specs=anywhere,
        input_output_aliases={0: 0},
        cost_estimate=pl.CostEstimate(flops=flops, bytes_accessed=0, transcendentals=0),
    )(x, *after)


def first_step(low, high, ahead, behind):
    half = low.shape[0]
    up, down = shifted(low, "y", NY, 1), shifted(high, "y", NY, -1)
    ahead = jnp.concatenate([ahead[:half] + up, ahead[half:]])
    return ahead, jnp.concatenate([behind[:half], behind[half:] + down])


def second_step(ahead, behind):
    return shifted(ahead, "y", NY, 1), shifted(behind, "y", NY, -1)


def added(own, up, down):
    return (own.astype(F32) + up.astype(F32) + down.astype(F32)).astype(BF16)


def summed_along_z(x):
    return lax.psum_scatter(x, "z", scatter_dimension=0, tiled=False)


def handing(odd):
    pairs = []
    for i in range(2 * 4 * NY * NZ):
        s, g, y, z = i // 128, i // 32 % 4, i // 8 % 4, i % 8
        pairs.append((i, (1 - s) * 128 + (g ^ (y // 2) ^ (2 * ((y + odd) % 2))) * 32 + g * 8 + z))
    return pairs


def handed_over(pair, group, y):
    swapped = y % 2 == 1
    one = jnp.where(swapped, pair[1], pair[0])
    two = jnp.where(swapped, pair[0], pair[1])
    one = lax.ppermute(one, AXES, handing(0))
    two = lax.ppermute(two, AXES, handing(1))
    turned = (group ^ y) >= 2
    return jnp.concatenate([jnp.where(turned, two, one), jnp.where(turned, one, two)])


def shards(hidden, down_weight, residual, norm_gain):
    h, w, gain = hidden[0], down_weight[0], norm_gain[0]
    xh, c, y, z = (lax.axis_index(a) for a in AXES[1:])
    group = xh * 2 + c
    part = lambda r: lax.dynamic_slice_in_dim(residual[0], (group ^ r) * 2048, 2048, axis=1)
    got = flipped(jnp.stack([part(1), part(3)]), "c")
    far_res = jnp.stack([part(2), got[1]])
    near_res = (part(0), got[0])
    m = y * NZ + z
    m = m.reshape(1)
    core = flipped(h, "c")
    (product_near,) = product(m, (h, core), w, near_res, 0, HALF, False, SCALE)
    far_res = flipped(far_res, "xh")
    near = summed_along_z(product_near)
    take = lambda j: lax.dynamic_index_in_dim(near, (y + j) % NY, axis=0, keepdims=False)
    opposite = take(2)
    sent = first_step(opposite[: HALF // 2], opposite[HALF // 2 :], take(1), take(-1))
    near = added(take(0), *second_step(*sent))
    steps, last = [], (product_near, far_res)
    for a, b in ORDER:
        x = h.reshape(2, HALF, -1)[:, a:b].reshape(2 * (b - a), -1)
        x = flipped(tied(x, near_res[1]) if a else x, "xh")
        x = tied(x, *last, flops=0 if a else TIE)
        low, high, rest = product(m, (x, flipped(x, "c")), w, far_res, a, b - a, True, 1 if a else FAR)
        last = (rest,)
        own, ahead, behind = rest
        steps.append((own, *first_step(low, high, ahead, behind)))
    (own, *one), (other, *two) = steps
    up, down = second_step(*one)
    one = added(own, up, down)
    sums = [one, added(tied(other, one, flops=HOLD), *second_step(*two))]
    sums = [lax.all_to_all(x, "z", split_axis=0, concat_axis=0, tiled=True) for x in sums]
    sums = [jnp.sum(x.astype(F32), axis=0).astype(BF16) for x in sums]
    handed = handed_over((near, jnp.concatenate(sums)), group, y)
    wide = handed.astype(F32)
    squares = jnp.sum(wide * wide, axis=1)
    squares = lax.all_to_all(
        jnp.broadcast_to(squares, (NY * NZ, 768)), ("y", "z"), split_axis=0, concat_axis=0, tiled=True
    )
    squares = jnp.sum(squares, axis=0)
    scale = lax.rsqrt(squares / D + 1e-05)
    normed = (wide * scale[:, None] * gain[None, :]).astype(BF16)
    return (handed[None], normed[None])


def solution(mesh):
    fine = Mesh(mesh.devices.reshape(2, 2, 2, NY, NZ), AXES)
    group, mp = ("xh", "c"), ("y", "z")
    return jax.shard_map(
        shards,
        mesh=fine,
        in_specs=(P("s", group, mp), P("s", mp, group), P("s", group + mp, None), P("s", mp)),
        out_specs=(P("s", group, mp), P("s", group, mp)),
        check_vma=False,
    )
```

```python
import functools

import jax
import jax.numpy as jnp
from jax import lax
from jax.experimental import pallas as pl
from jax.experimental.pallas import tpu as pltpu
from jax.sharding import Mesh
from jax.sharding import PartitionSpec as P

D = 8192
NZ, NY = 8, 4
COLS = 256
STEP = 2
HALF = 384
ORDER = ((0, 192), (192, HALF))
HOLD = 1 * 10**10
TIE = 3 * 10**11
SCALE, FAR = 20, 1
VMEM = 50 * 2**20
AXES = ("s", "xh", "c", "y", "z")
F32, BF16 = jnp.float32, jnp.bfloat16


def shifted(x, axis, n, by):
    return lax.ppermute(x, axis, [(i, (i + by) % n) for i in range(n)])


def flipped(x, *axes):
    n = 2 ** len(axes)
    return lax.ppermute(x, axes, [(i, n - 1 - i) for i in range(n)])


def product_kernel(first, rows, relative, m_ref, h0_ref, h1_ref, w_ref, r0_ref, r1_ref, *out_refs):
    m = m_ref[0]
    step = pl.program_id(0)
    parts = [slice(k * COLS, (k + 1) * COLS) for k in range(STEP)]

    def at_owner(owner, k, use):
        if not relative:
            use(out_refs[0], (k, owner))
            return
        low_ref, high_ref, rest_ref = out_refs
        ahead = lax.rem(owner - m // NZ + NY, NY)
        pl.when(ahead != 2)(lambda: use(rest_ref, (jnp.where(ahead == 3, 2, ahead), k)))
        early = step < NZ // STEP // 2
        pl.when((ahead == 2) & early)(lambda: use(low_ref, (k,)))
        pl.when((ahead == 2) & jnp.logical_not(early))(lambda: use(high_ref, (k,)))

    for i, h_ref in enumerate((h0_ref, h1_ref)):
        acc = jnp.dot(h_ref[...], w_ref[...], preferred_element_type=F32).astype(BF16)
        for half in range(2):
            for k, part in enumerate(parts):

                def store(ref, at, value=acc[half * rows : (half + 1) * rows, part]):
                    ref[at] = value

                at_owner(i * 2 + half, k, store)

    row = m % 16 * 24

    @pl.when((row >= first) & (row < first + rows))
    def _():
        window = pl.ds(pl.multiple_of(row // 16 * 16 - first, 16), 32)
        for i, r_ref in enumerate((r0_ref, r1_ref)):
            none = jnp.zeros((8, COLS), F32)
            for k, part in enumerate(parts):
                r = r_ref[:, part].astype(F32)
                late, soon = jnp.concatenate([none, r]), jnp.concatenate([r, none])

                def add(ref, at, value=jnp.where(row % 16 == 8, late, soon)):
                    at = at + (window, slice(None))
                    ref[at] = (ref[at].astype(F32) + value).astype(BF16)

                at_owner(i * 2 + m // 16, k, add)


def product(m, h, w, res, first, rows, relative, scale=1):
    whole = lambda j: (0, 0)
    columns = lambda j: (0, j)
    if relative:
        last = NZ // STEP // 2 - 1
        out = [
            ((NZ // 2, rows, COLS), (STEP, rows, COLS), lambda j: (jnp.minimum(j, last), 0, 0)),
            ((NZ // 2, rows, COLS), (STEP, rows, COLS), lambda j: (jnp.maximum(j - last - 1, 0), 0, 0)),
            ((3, NZ, rows, COLS), (3, STEP, rows, COLS), lambda j: (0, j, 0, 0)),
        ]
    else:
        out = [((NZ, NY, rows, COLS), (STEP, NY, rows, COLS), lambda j: (j, 0, 0, 0))]
    return pl.pallas_call(
        functools.partial(product_kernel, first, rows, relative),
        out_shape=[jax.ShapeDtypeStruct(shape, BF16) for shape, _, _ in out],
        grid=(NZ // STEP,),
        in_specs=[
            pl.BlockSpec(memory_space=pltpu.SMEM),
            pl.BlockSpec(h[0].shape, whole),
            pl.BlockSpec(h[1].shape, whole),
            pl.BlockSpec((w.shape[0], STEP * COLS), columns),
            pl.BlockSpec((24, STEP * COLS), columns),
            pl.BlockSpec((24, STEP * COLS), columns),
        ],
        out_specs=[pl.BlockSpec(block, place) for _, block, place in out],
        compiler_params=pltpu.CompilerParams(vmem_limit_bytes=VMEM),
        cost_estimate=pl.CostEstimate(
            flops=scale * 2 * NY * rows * w.size,
            bytes_accessed=2 * (NY * rows * NZ * COLS + w.size + 2 * h[0].size),
            transcendentals=0,
        ),
    )(m, h[0], h[1], w, res[0], res[1])


def tied(x, *after, flops=0):
    anywhere = pl.BlockSpec(memory_space=pl.ANY)
    return pl.pallas_call(
        lambda *refs: None,
        out_shape=jax.ShapeDtypeStruct(x.shape, x.dtype),
        in_specs=[anywhere] * (1 + len(after)),
        out_specs=anywhere,
        input_output_aliases={0: 0},
        cost_estimate=pl.CostEstimate(flops=flops, bytes_accessed=0, transcendentals=0),
    )(x, *after)


def first_step(low, high, ahead, behind):
    half = low.shape[0]
    up, down = shifted(low, "y", NY, 1), shifted(high, "y", NY, -1)
    ahead = jnp.concatenate([ahead[:half] + up, ahead[half:]])
    return ahead, jnp.concatenate([behind[:half], behind[half:] + down])


def second_step(ahead, behind):
    return shifted(ahead, "y", NY, 1), shifted(behind, "y", NY, -1)


def ring_summed_along_z(x, z):
    piece = lambda j: lax.dynamic_index_in_dim(x, (z + j) % NZ, axis=0, keepdims=False)
    far, half = piece(NZ // 2), COLS // 2
    up, down = shifted(far[:, :half], "z", NZ, 1), shifted(far[:, half:], "z", NZ, -1)
    ahead, behind = piece(3), piece(-3)
    ahead = jnp.concatenate([ahead[:, :half] + up, ahead[:, half:]], axis=1)
    behind = jnp.concatenate([behind[:, :half], behind[:, half:] + down], axis=1)
    for j in (2, 1, 0):
        up, down = shifted(ahead, "z", NZ, 1), shifted(behind, "z", NZ, -1)
        if j:
            ahead, behind = piece(j) + up, piece(-j) + down
    return added(piece(0), up, down)


def added(own, up, down):
    return (own.astype(F32) + up.astype(F32) + down.astype(F32)).astype(BF16)


def summed_along_z(x):
    return lax.psum_scatter(x, "z", scatter_dimension=0, tiled=False)


def handing(odd):
    pairs = []
    for i in range(2 * 4 * NY * NZ):
        s, g, y, z = i // 128, i // 32 % 4, i // 8 % 4, i % 8
        pairs.append((i, (1 - s) * 128 + (g ^ (y // 2) ^ (2 * ((y + odd) % 2))) * 32 + g * 8 + z))
    return pairs


def handed_over(pair, group, y):
    swapped = y % 2 == 1
    one = jnp.where(swapped, pair[1], pair[0])
    two = jnp.where(swapped, pair[0], pair[1])
    one = lax.ppermute(one, AXES, handing(0))
    two = lax.ppermute(two, AXES, handing(1))
    turned = (group ^ y) >= 2
    return jnp.concatenate([jnp.where(turned, two, one), jnp.where(turned, one, two)])


def shards(hidden, down_weight, residual, norm_gain):
    h, w, gain = hidden[0], down_weight[0], norm_gain[0]
    xh, c, y, z = (lax.axis_index(a) for a in AXES[1:])
    group = xh * 2 + c
    part = lambda r: lax.dynamic_slice_in_dim(residual[0], (group ^ r) * 2048, 2048, axis=1)
    got = flipped(jnp.stack([part(1), part(3)]), "c")
    far_res = jnp.stack([part(2), got[1]])
    near_res = (part(0), got[0])
    m = y * NZ + z
    m = m.reshape(1)
    core = flipped(h, "c")
    (product_near,) = product(m, (h, core), w, near_res, 0, HALF, False, SCALE)
    far_res = flipped(far_res, "xh")
    near = summed_along_z(product_near)
    take = lambda j: lax.dynamic_index_in_dim(near, (y + j) % NY, axis=0, keepdims=False)
    opposite = take(2)
    sent = first_step(opposite[: HALF // 2], opposite[HALF // 2 :], take(1), take(-1))
    near = added(take(0), *second_step(*sent))
    steps, last = [], (product_near, far_res)
    for a, b in ORDER:
        x = h.reshape(2, HALF, -1)[:, a:b].reshape(2 * (b - a), -1)
        x = flipped(tied(x, near_res[1]) if a else x, "xh")
        x = tied(x, *last, flops=0 if a else TIE)
        low, high, rest = product(m, (x, flipped(x, "c")), w, far_res, a, b - a, True, 1 if a else FAR)
        last = (rest,)
        own, ahead, behind = rest
        steps.append((own, *first_step(low, high, ahead, behind)))
    (own, *one), (other, *two) = steps
    up, down = second_step(*one)
    one = added(own, up, down)
    other = added(tied(other, one, flops=HOLD), *second_step(*two))
    other = lax.all_to_all(other, "z", split_axis=0, concat_axis=0, tiled=True)
    other = jnp.sum(other.astype(F32), axis=0).astype(BF16)
    sums = [ring_summed_along_z(one, z), other]
    handed = handed_over((near, jnp.concatenate(sums)), group, y)
    wide = handed.astype(F32)
    squares = jnp.sum(wide * wide, axis=1)
    squares = lax.all_to_all(
        jnp.broadcast_to(squares, (NY * NZ, 768)), ("y", "z"), split_axis=0, concat_axis=0, tiled=True
    )
    squares = jnp.sum(squares, axis=0)
    scale = lax.rsqrt(squares / D + 1e-05)
    normed = (wide * scale[:, None] * gain[None, :]).astype(BF16)
    return (handed[None], normed[None])


def solution(mesh):
    fine = Mesh(mesh.devices.reshape(2, 2, 2, NY, NZ), AXES)
    group, mp = ("xh", "c"), ("y", "z")
    return jax.shard_map(
        shards,
        mesh=fine,
        in_specs=(P("s", group, mp), P("s", mp, group), P("s", group + mp, None), P("s", mp)),
        out_specs=(P("s", group, mp), P("s", group, mp)),
        check_vma=False,
    )
```

```python
import functools

import jax
import jax.numpy as jnp
from jax import lax
from jax.experimental import pallas as pl
from jax.experimental.pallas import tpu as pltpu
from jax.sharding import Mesh
from jax.sharding import PartitionSpec as P

D = 8192
NZ, NY = 8, 4
COLS = 256
STEP = 2
HALF = 384
ORDER = ((0, 192), (192, HALF))
TIE = 3 * 10**11
SCALE, FAR = 20, 1
VMEM = 50 * 2**20
AXES = ("s", "xh", "c", "y", "z")
F32, BF16 = jnp.float32, jnp.bfloat16


def shifted(x, axis, n, by):
    return lax.ppermute(x, axis, [(i, (i + by) % n) for i in range(n)])


def flipped(x, *axes):
    n = 2 ** len(axes)
    return lax.ppermute(x, axes, [(i, n - 1 - i) for i in range(n)])


def product_kernel(first, rows, y_major, m_ref, h0_ref, h1_ref, w_ref, r0_ref, r1_ref, *refs):
    out_ref = refs[-1]

    def block(i, half, k):
        return (i * 2 + half, k) if y_major else (k, i * 2 + half)

    parts = [slice(k * COLS, (k + 1) * COLS) for k in range(STEP)]
    for i, h_ref in enumerate((h0_ref, h1_ref)):
        for half in range(2):
            at = half * rows
            acc = jnp.dot(h_ref[at : at + rows], w_ref[...], preferred_element_type=F32)
            for k, part in enumerate(parts):
                out_ref[block(i, half, k)] = acc[:, part].astype(BF16)

    m = m_ref[0]
    row = m % 16 * 24

    @pl.when((row >= first) & (row < first + rows))
    def _():
        window = pl.ds(pl.multiple_of(row // 16 * 16 - first, 16), 32)
        for i, r_ref in enumerate((r0_ref, r1_ref)):
            none = jnp.zeros((8, COLS), F32)
            for k, part in enumerate(parts):
                r = r_ref[:, part].astype(F32)
                late, soon = jnp.concatenate([none, r]), jnp.concatenate([r, none])
                at = block(i, m // 16, k) + (window, slice(None))
                out_ref[at] = (out_ref[at].astype(F32) + jnp.where(row % 16 == 8, late, soon)).astype(BF16)


def product(m, h, w, res, first, rows, y_major, scale=1, after=()):
    whole = lambda j: (0, 0)
    columns = lambda j: (0, j)
    if y_major:
        shape, block, place = (NY, NZ, rows, COLS), (NY, STEP, rows, COLS), lambda j: (0, j, 0, 0)
    else:
        shape, block, place = (NZ, NY, rows, COLS), (STEP, NY, rows, COLS), lambda j: (j, 0, 0, 0)
    return pl.pallas_call(
        functools.partial(product_kernel, first, rows, y_major),
        out_shape=jax.ShapeDtypeStruct(shape, BF16),
        grid=(NZ // STEP,),
        in_specs=[
            pl.BlockSpec(memory_space=pltpu.SMEM),
            pl.BlockSpec(h[0].shape, whole),
            pl.BlockSpec(h[1].shape, whole),
            pl.BlockSpec((w.shape[0], STEP * COLS), columns),
            pl.BlockSpec((24, STEP * COLS), columns),
            pl.BlockSpec((24, STEP * COLS), columns),
        ]
        + [pl.BlockSpec(memory_space=pl.ANY)] * len(after),
        out_specs=pl.BlockSpec(block, place),
        compiler_params=pltpu.CompilerParams(vmem_limit_bytes=VMEM),
        cost_estimate=pl.CostEstimate(
            flops=scale * 2 * NY * rows * w.size,
            bytes_accessed=2 * (NY * rows * NZ * COLS + w.size + 2 * h[0].size),
            transcendentals=0,
        ),
    )(m, h[0], h[1], w, res[0], res[1], *after)


def tied(x, *after, flops=0):
    anywhere = pl.BlockSpec(memory_space=pl.ANY)
    return pl.pallas_call(
        lambda *refs: None,
        out_shape=jax.ShapeDtypeStruct(x.shape, x.dtype),
        in_specs=[anywhere] * (1 + len(after)),
        out_specs=anywhere,
        input_output_aliases={0: 0},
        cost_estimate=pl.CostEstimate(flops=flops, bytes_accessed=0, transcendentals=0),
    )(x, *after)


def summed_along_y(x, y):
    half = x.shape[1] // 2
    take = lambda j: lax.dynamic_index_in_dim(x, (y + j) % NY, axis=0, keepdims=False)
    far, ahead, behind = take(2), take(1), take(-1)
    up, down = shifted(far[:half], "y", NY, 1), shifted(far[half:], "y", NY, -1)
    ahead = jnp.concatenate([ahead[:half] + up, ahead[half:]])
    behind = jnp.concatenate([behind[:half], behind[half:] + down])
    up, down = shifted(ahead, "y", NY, 1), shifted(behind, "y", NY, -1)
    return take(0).astype(F32) + up.astype(F32) + down.astype(F32)


def summed_along_z(x):
    return lax.psum_scatter(x, "z", scatter_dimension=0, tiled=False)


def handing(odd):
    pairs = []
    for i in range(2 * 4 * NY * NZ):
        s, g, y, z = i // 128, i // 32 % 4, i // 8 % 4, i % 8
        pairs.append((i, (1 - s) * 128 + (g ^ (y // 2) ^ (2 * ((y + odd) % 2))) * 32 + g * 8 + z))
    return pairs


def handed_over(pair, group, y):
    swapped = y % 2 == 1
    one = jnp.where(swapped, pair[1], pair[0])
    two = jnp.where(swapped, pair[0], pair[1])
    one = lax.ppermute(one, AXES, handing(0))
    two = lax.ppermute(two, AXES, handing(1))
    turned = (group ^ y) >= 2
    return jnp.concatenate([jnp.where(turned, two, one), jnp.where(turned, one, two)])


def shards(hidden, down_weight, residual, norm_gain):
    h, w, gain = hidden[0], down_weight[0], norm_gain[0]
    xh, c, y, z = (lax.axis_index(a) for a in AXES[1:])
    group = xh * 2 + c
    part = lambda r: lax.dynamic_slice_in_dim(residual[0], (group ^ r) * 2048, 2048, axis=1)
    got = flipped(jnp.stack([part(1), part(3)]), "c")
    far_res = jnp.stack([part(2), got[1]])
    near_res = (part(0), got[0])
    m = y * NZ + z
    m = m.reshape(1)
    core = flipped(h, "c")
    product_near = product(m, (h, core), w, near_res, 0, HALF, False, SCALE)
    far_res = flipped(far_res, "xh")
    near = summed_along_y(summed_along_z(product_near), y).astype(BF16)
    sums, last = [], product_near
    for a, b in ORDER:
        x = h.reshape(2, HALF, -1)[:, a:b].reshape(2 * (b - a), -1)
        x = flipped(tied(x, near_res[1]) if a else x, "xh")
        x = tied(x, last, flops=0 if a else TIE)
        x = last = product(m, (x, flipped(x, "c")), w, far_res, a, b - a, True, 1 if a else FAR)
        x = summed_along_y(x, y).astype(BF16)
        x = lax.all_to_all(x, "z", split_axis=0, concat_axis=0, tiled=True)
        sums.append(jnp.sum(x.astype(F32), axis=0).astype(BF16))
    handed = handed_over((near, jnp.concatenate(sums)), group, y)
    wide = handed.astype(F32)
    squares = jnp.sum(wide * wide, axis=1)
    squares = lax.all_to_all(
        jnp.broadcast_to(squares, (NY * NZ, 768)), ("y", "z"), split_axis=0, concat_axis=0, tiled=True
    )
    scale = lax.rsqrt(jnp.sum(squares, axis=0) / D + 1e-05)
    normed = (wide * scale[:, None] * gain[None, :]).astype(BF16)
    return (handed[None], normed[None])


def solution(mesh):
    fine = Mesh(mesh.devices.reshape(2, 2, 2, NY, NZ), AXES)
    group, mp = ("xh", "c"), ("y", "z")
    return jax.shard_map(
        shards,
        mesh=fine,
        in_specs=(P("s", group, mp), P("s", mp, group), P("s", group + mp, None), P("s", mp)),
        out_specs=(P("s", group, mp), P("s", group, mp)),
        check_vma=False,
    )
```

```python
import functools

import jax
import jax.numpy as jnp
from jax import lax
from jax.experimental import pallas as pl
from jax.experimental.pallas import tpu as pltpu
from jax.sharding import Mesh
from jax.sharding import PartitionSpec as P

D = 8192
NZ, NY = 8, 4
COLS = 256
STEP = 2
HALF = 384
ORDER = ((0, 192), (192, HALF))
TIE = 3 * 10**11
SCALE, FAR = 20, 1
VMEM = 50 * 2**20
AXES = ("s", "xh", "c", "y", "z")
F32, BF16 = jnp.float32, jnp.bfloat16


def shifted(x, axis, n, by):
    return lax.ppermute(x, axis, [(i, (i + by) % n) for i in range(n)])


def flipped(x, *axes):
    n = 2 ** len(axes)
    return lax.ppermute(x, axes, [(i, n - 1 - i) for i in range(n)])


def product_kernel(first, rows, relative, m_ref, h0_ref, h1_ref, w_ref, r0_ref, r1_ref, *out_refs):
    m = m_ref[0]
    step = pl.program_id(0)
    parts = [slice(k * COLS, (k + 1) * COLS) for k in range(STEP)]

    def at_owner(owner, k, use):
        if not relative:
            use(out_refs[0], (k, owner))
            return
        low_ref, high_ref, rest_ref = out_refs
        ahead = lax.rem(owner - m // NZ + NY, NY)
        pl.when(ahead != 2)(lambda: use(rest_ref, (jnp.where(ahead == 3, 2, ahead), k)))
        early = step < NZ // STEP // 2
        pl.when((ahead == 2) & early)(lambda: use(low_ref, (k,)))
        pl.when((ahead == 2) & jnp.logical_not(early))(lambda: use(high_ref, (k,)))

    for i, h_ref in enumerate((h0_ref, h1_ref)):
        acc = jnp.dot(h_ref[...], w_ref[...], preferred_element_type=F32).astype(BF16)
        for half in range(2):
            for k, part in enumerate(parts):

                def store(ref, at, value=acc[half * rows : (half + 1) * rows, part]):
                    ref[at] = value

                at_owner(i * 2 + half, k, store)

    row = m % 16 * 24

    @pl.when((row >= first) & (row < first + rows))
    def _():
        window = pl.ds(pl.multiple_of(row // 16 * 16 - first, 16), 32)
        for i, r_ref in enumerate((r0_ref, r1_ref)):
            none = jnp.zeros((8, COLS), F32)
            for k, part in enumerate(parts):
                r = r_ref[:, part].astype(F32)
                late, soon = jnp.concatenate([none, r]), jnp.concatenate([r, none])

                def add(ref, at, value=jnp.where(row % 16 == 8, late, soon)):
                    at = at + (window, slice(None))
                    ref[at] = (ref[at].astype(F32) + value).astype(BF16)

                at_owner(i * 2 + m // 16, k, add)


def product(m, h, w, res, first, rows, relative, scale=1):
    whole = lambda j: (0, 0)
    columns = lambda j: (0, j)
    if relative:
        last = NZ // STEP // 2 - 1
        out = [
            ((NZ // 2, rows, COLS), (STEP, rows, COLS), lambda j: (jnp.minimum(j, last), 0, 0)),
            ((NZ // 2, rows, COLS), (STEP, rows, COLS), lambda j: (jnp.maximum(j - last - 1, 0), 0, 0)),
            ((3, NZ, rows, COLS), (3, STEP, rows, COLS), lambda j: (0, j, 0, 0)),
        ]
    else:
        out = [((NZ, NY, rows, COLS), (STEP, NY, rows, COLS), lambda j: (j, 0, 0, 0))]
    return pl.pallas_call(
        functools.partial(product_kernel, first, rows, relative),
        out_shape=[jax.ShapeDtypeStruct(shape, BF16) for shape, _, _ in out],
        grid=(NZ // STEP,),
        in_specs=[
            pl.BlockSpec(memory_space=pltpu.SMEM),
            pl.BlockSpec(h[0].shape, whole),
            pl.BlockSpec(h[1].shape, whole),
            pl.BlockSpec((w.shape[0], STEP * COLS), columns),
            pl.BlockSpec((24, STEP * COLS), columns),
            pl.BlockSpec((24, STEP * COLS), columns),
        ],
        out_specs=[pl.BlockSpec(block, place) for _, block, place in out],
        compiler_params=pltpu.CompilerParams(vmem_limit_bytes=VMEM),
        cost_estimate=pl.CostEstimate(
            flops=scale * 2 * NY * rows * w.size,
            bytes_accessed=2 * (NY * rows * NZ * COLS + w.size + 2 * h[0].size),
            transcendentals=0,
        ),
    )(m, h[0], h[1], w, res[0], res[1])


def tied(x, *after, flops=0):
    anywhere = pl.BlockSpec(memory_space=pl.ANY)
    return pl.pallas_call(
        lambda *refs: None,
        out_shape=jax.ShapeDtypeStruct(x.shape, x.dtype),
        in_specs=[anywhere] * (1 + len(after)),
        out_specs=anywhere,
        input_output_aliases={0: 0},
        cost_estimate=pl.CostEstimate(flops=flops, bytes_accessed=0, transcendentals=0),
    )(x, *after)


def first_step(low, high, ahead, behind):
    half = low.shape[0]
    up, down = shifted(low, "y", NY, 1), shifted(high, "y", NY, -1)
    ahead = jnp.concatenate([ahead[:half] + up, ahead[half:]])
    return ahead, jnp.concatenate([behind[:half], behind[half:] + down])


def second_step(ahead, behind):
    return shifted(ahead, "y", NY, 1), shifted(behind, "y", NY, -1)


def added(own, up, down):
    return (own.astype(F32) + up.astype(F32) + down.astype(F32)).astype(BF16)


def summed_along_z(x):
    return lax.psum_scatter(x, "z", scatter_dimension=0, tiled=False)


def handing(odd):
    pairs = []
    for i in range(2 * 4 * NY * NZ):
        s, g, y, z = i // 128, i // 32 % 4, i // 8 % 4, i % 8
        pairs.append((i, (1 - s) * 128 + (g ^ (y // 2) ^ (2 * ((y + odd) % 2))) * 32 + g * 8 + z))
    return pairs


def handed_over(pair, group, y):
    swapped = y % 2 == 1
    one = jnp.where(swapped, pair[1], pair[0])
    two = jnp.where(swapped, pair[0], pair[1])
    one = lax.ppermute(one, AXES, handing(0))
    two = lax.ppermute(two, AXES, handing(1))
    turned = (group ^ y) >= 2
    return jnp.concatenate([jnp.where(turned, two, one), jnp.where(turned, one, two)])


def shards(hidden, down_weight, residual, norm_gain):
    h, w, gain = hidden[0], down_weight[0], norm_gain[0]
    xh, c, y, z = (lax.axis_index(a) for a in AXES[1:])
    group = xh * 2 + c
    part = lambda r: lax.dynamic_slice_in_dim(residual[0], (group ^ r) * 2048, 2048, axis=1)
    got = flipped(jnp.stack([part(1), part(3)]), "c")
    far_res = jnp.stack([part(2), got[1]])
    near_res = (part(0), got[0])
    m = y * NZ + z
    m = m.reshape(1)
    core = flipped(h, "c")
    (product_near,) = product(m, (h, core), w, near_res, 0, HALF, False, SCALE)
    far_res = flipped(far_res, "xh")
    near = summed_along_z(product_near)
    take = lambda j: lax.dynamic_index_in_dim(near, (y + j) % NY, axis=0, keepdims=False)
    opposite = take(2)
    sent = first_step(opposite[: HALF // 2], opposite[HALF // 2 :], take(1), take(-1))
    near = added(take(0), *second_step(*sent))
    steps, last = [], (product_near, far_res)
    for a, b in ORDER:
        x = h.reshape(2, HALF, -1)[:, a:b].reshape(2 * (b - a), -1)
        x = flipped(tied(x, near_res[1]) if a else x, "xh")
        x = tied(x, *last, flops=0 if a else TIE)
        low, high, rest = product(m, (x, flipped(x, "c")), w, far_res, a, b - a, True, 1 if a else FAR)
        last = (rest,)
        own, ahead, behind = rest
        steps.append((own, *first_step(low, high, ahead, behind)))
    (own, *one), (other, *two) = steps
    up, down = second_step(*one)
    one = added(own, up, down)
    sums = [one, added(other, *second_step(*two))]
    sums = [lax.all_to_all(x, "z", split_axis=0, concat_axis=0, tiled=True) for x in sums]
    sums = [jnp.sum(x.astype(F32), axis=0).astype(BF16) for x in sums]
    handed = handed_over((near, jnp.concatenate(sums)), group, y)
    wide = handed.astype(F32)
    squares = jnp.sum(wide * wide, axis=1)
    squares = lax.all_to_all(
        jnp.broadcast_to(squares, (NY * NZ, 768)), ("y", "z"), split_axis=0, concat_axis=0, tiled=True
    )
    squares = jnp.sum(squares, axis=0)
    scale = lax.rsqrt(squares / D + 1e-05)
    normed = (wide * scale[:, None] * gain[None, :]).astype(BF16)
    return (handed[None], normed[None])


def solution(mesh):
    fine = Mesh(mesh.devices.reshape(2, 2, 2, NY, NZ), AXES)
    group, mp = ("xh", "c"), ("y", "z")
    return jax.shard_map(
        shards,
        mesh=fine,
        in_specs=(P("s", group, mp), P("s", mp, group), P("s", group + mp, None), P("s", mp)),
        out_specs=(P("s", group, mp), P("s", group, mp)),
        check_vma=False,
    )
```
